32 devices in a mesh: rep: 2 (over x), node: 2 (over core), dev: 8 (over z, y).
Axes of the slice: x: 2, y: 2, z: 4, core: 2. Of those that a mesh axis runs over, the one named last changes fastest.
Arguments:
- tokens: bfloat16 [1024, 7168], P(('rep', 'node', 'dev')), parts along dimension 0, may hold values from -6 to 6
- expert_picks: int32 [1024, 2], P(('rep', 'node', 'dev')), parts along dimension 0, may hold values from 0 to 3, all different within a row; in each aligned block of 32 rows (0 to 31, 32 to 63, ...) at most 32 rows name the same one
- mix_weights: float32 [1024, 2], P(('rep', 'node', 'dev')), parts along dimension 0, may hold values from 0.2 to 1
- w_gate: bfloat16 [7168, 4096], P(None, ('node', 'dev')), may hold values from -0.0625 to 0.0625
- w_up: bfloat16 [7168, 4096], P(None, ('node', 'dev')), may hold values from -0.0625 to 0.0625
- w_down: bfloat16 [4096, 7168], P(('node', 'dev')), may hold values from -0.1875 to 0.1875
Outputs:
- mixed: bfloat16 [1024, 7168], P(('rep', 'node', 'dev')), parts along dimension 0
The draws below stay inside these ranges and needn't reach their ends.
There are 2 independent parts, one for each index of `rep`. The reference program is written for one: setup_inputs(seed, part) draws one part's arguments, and reference() takes and returns one part's arrays. A program takes and returns all parts, laid end to end along the dimension named above; an argument that names none is the same for every part. Nothing has to cross between parts.
Inputs may be any that keep to these rules, and one draw needn't show every extreme that they name: `expert_picks`: A row's 2 picks name different experts; in each aligned block of 32 rows (the rows of one device) no expert is named by more than 32 rows, a bound that some block reaches.
All inputs are finite; a program needn't handle non-finite values.
Results may differ from the reference program's by a relative error of at most 0.0064.
Values may be sent and summed in bfloat16 or wider, within the bound.
A program may use at most 128 MiB of HBM per device.

```python
import math
import jax
import jax.numpy as jnp
import numpy as np
from jax import lax

D = 7168
FF = 1024
SHARDS = 4
TOPK = 2
TOK_DEV = 32
FF_DEV = 256
EXPERTS = 4
CAP = 32
TOKENS = 512


def shard_levels(rng, shape, cuts, smallest, top_value):
    def one(dim, blocks):
        heights = jax.random.uniform(jax.random.fold_in(jax.random.fold_in(rng, 6), dim), (blocks,), jnp.float32, smallest / len(cuts), top_value / len(cuts))
        return jnp.repeat(jnp.exp(heights), shape[dim] // blocks).reshape((-1,) + (1,) * (len(shape) - dim - 1))

    gain = one(*cuts[0])
    for cut in cuts[1:]:
        gain = gain * one(*cut)
    return gain


def assign_block(stream_key, own, number, rows, amount, top, most, skew):
    order = jax.random.permutation(stream_key, amount)
    heavy_load, common = load_shares(amount, rows * top, most, skew, True), load_shares(amount, rows * top, most, skew, False)
    places = jnp.arange(amount)

    def named(lengths, turn):
        used = int((lengths > 0).sum())
        fixed = max(1, used // 4)
        shifted = fixed + (places - fixed + turn * (used - fixed)) % max(1, amount - fixed)
        return jnp.zeros((amount,), jnp.int32).at[order[jnp.where(places < fixed, places, shifted)]].set(jnp.asarray(lengths, jnp.int32))

    lengths = jnp.where(number % 4 == 0, named(heavy_load, number // 4), named(common, number - number // 4 - 1))
    mixed = jax.random.permutation(jax.random.fold_in(own, 3), amount)
    giver, taker = mixed[0:amount // 2 * 2:2], mixed[1:amount // 2 * 2:2]
    room = jnp.minimum(lengths[giver] - 1, most - lengths[taker]) // 2
    room = jnp.where((giver == order[0]) | (taker == order[0]) | (lengths[taker] == 0), 0, jnp.maximum(room, 0))
    shifted = jax.random.randint(jax.random.fold_in(own, 4), (amount // 2,), 0, 1 << 20) % (room + 1)
    lengths = lengths.at[giver].add(-shifted).at[taker].add(shifted)
    labels = jnp.searchsorted(jnp.cumsum(lengths), jnp.arange(rows * top), side="right").astype(jnp.int32)
    grid = labels.reshape(top, rows).T
    grid = grid[jax.random.permutation(jax.random.fold_in(own, 1), rows)]
    turn = jax.random.randint(jax.random.fold_in(own, 2), (rows, 1), 0, top)
    return jnp.take_along_axis(grid, (jnp.arange(top)[None, :] + turn) % top, axis=1)


def load_shares(count, total, most, slope, full):
    loads = [(1 << 20) // math.isqrt(standing ** slope) + 1 for standing in range(1, count + 1)]
    largest = most if full else min(most, max(-(-total // count), total * loads[0] // sum(loads)))
    least = 1 if total - largest >= count - 1 else 0
    holding, surplus = [largest] + [least] * (count - 1), total - largest - least * (count - 1)
    while surplus > 0:
        free = [i for i in range(1, count) if holding[i] < largest] or [i for i in range(1, count) if holding[i] < most]
        pool, remaining = sum([loads[i] for i in free]), surplus
        for i in free:
            addition = min(most - holding[i], max(1, remaining * loads[i] // pool), surplus)
            holding[i] = holding[i] + addition
            surplus = surplus - addition
    return np.array(holding)


def bell_draw(own_key, extent, width, limit, pieces=(), kind=jnp.bfloat16):
    level = shard_levels(own_key, extent, pieces, -0.22, 0.18) if pieces else 1.0
    values = jax.random.normal(own_key, extent, jnp.float32) * width * level
    return jnp.minimum(jnp.maximum(values, -limit), limit).astype(kind)


def setup_inputs(seed: int = 0, part: int = 0) -> dict:
    arg_keys = jax.random.split(jax.random.key(seed), 7)
    own_keys = jax.random.split(jax.random.fold_in(arg_keys[6], part), 7)
    tokens = bell_draw(own_keys[0], (TOKENS, D), 1.0, 6.0, ((0, 16),))
    expert_picks_keys = jax.random.split(jax.random.fold_in(own_keys[1], 1), TOKENS // TOK_DEV)
    expert_picks_turns = jax.random.permutation(jax.random.fold_in(own_keys[1], 3), TOKENS // TOK_DEV)
    expert_picks = jax.vmap(lambda own, number: assign_block(jax.random.fold_in(own_keys[1], 2), own, number, TOK_DEV, EXPERTS, TOPK, CAP, 2))(expert_picks_keys, expert_picks_turns).reshape((TOKENS, TOPK))
    mix_weights = jnp.clip(0.2 + 0.8 * jax.random.uniform(own_keys[2], (TOKENS, TOPK), jnp.float32) ** shard_levels(own_keys[2], (TOKENS, TOPK), ((0, 16),), -0.2, 0.2), 0.2, 1.0)
    w_gate = bell_draw(arg_keys[3], (D, EXPERTS * FF), D ** -0.5, 0.0625, ((1, 16),))
    w_up = bell_draw(arg_keys[4], (D, EXPERTS * FF), D ** -0.5, 0.0625, ((1, 16),))
    w_down = bell_draw(arg_keys[5], (EXPERTS * FF, D), FF ** -0.5, 0.1875, ((0, 16),))
    return {"tokens": tokens, "expert_picks": expert_picks, "mix_weights": mix_weights, "w_gate": w_gate, "w_up": w_up, "w_down": w_down}


def reference(tokens, expert_picks, mix_weights, w_gate, w_up, w_down):
    sources = EXPERTS * SHARDS
    picks_flat = expert_picks.reshape(-1).astype(jnp.int32)
    onehot = (picks_flat[:, None] == jnp.arange(EXPERTS, dtype=jnp.int32)[None, :]).astype(jnp.int32)
    blocks = onehot.reshape(sources, TOK_DEV * TOPK, EXPERTS)
    ranking = (jnp.cumsum(blocks, axis=1) - blocks).reshape(-1, EXPERTS)
    position = jnp.sum(ranking * onehot, axis=1).astype(jnp.int32)
    source_id = (jnp.arange(TOKENS * TOPK, dtype=jnp.int32) // (TOK_DEV * TOPK)).astype(jnp.int32)
    slot_index = ((picks_flat * sources + source_id) * CAP + position).astype(jnp.int32)
    repeated = jnp.repeat(tokens, TOPK, axis=0)
    buffer = jnp.zeros((EXPERTS * sources * CAP, D), jnp.bfloat16).at[slot_index].set(repeated)
    buffer = buffer.reshape(EXPERTS, sources * CAP, D)

    def run_expert(inputs):
        rows_in, expert_id = inputs
        start = (expert_id * FF).astype(jnp.int32)
        gate_cols = lax.dynamic_slice_in_dim(w_gate, start, FF, 1)
        up_cols = lax.dynamic_slice_in_dim(w_up, start, FF, 1)
        down_rows = lax.dynamic_slice_in_dim(w_down, start, FF, 0)
        gate_proj = jnp.dot(rows_in, gate_cols, preferred_element_type=jnp.float32)
        up_proj = jnp.dot(rows_in, up_cols, preferred_element_type=jnp.float32)
        hidden = (jax.nn.silu(gate_proj) * up_proj).astype(jnp.bfloat16)
        summed = jnp.zeros((rows_in.shape[0], D), jnp.float32)
        for shard_id in range(SHARDS):
            lower = shard_id * FF_DEV
            shard_out = jnp.dot(hidden[:, lower:lower + FF_DEV], down_rows[lower:lower + FF_DEV],
                                preferred_element_type=jnp.float32).astype(jnp.bfloat16)
            summed = summed + shard_out.astype(jnp.float32)
        return summed.astype(jnp.bfloat16)

    expert_out = lax.map(run_expert, (buffer, jnp.arange(EXPERTS, dtype=jnp.int32))).reshape(-1, D)
    picked = expert_out[slot_index].astype(jnp.float32).reshape(TOKENS, TOPK, D)
    weighted = picked * mix_weights.astype(jnp.float32)[:, :, None]
    return jnp.sum(weighted, axis=1).astype(jnp.bfloat16)
```

```python
import functools

import jax
import jax.numpy as jnp
from jax import lax
from jax.experimental import pallas as pl
from jax.experimental.pallas import tpu as pltpu
from jax.sharding import PartitionSpec as P

SHARDS = 4
LANES = 128
MESH = pl.DeviceIdType.MESH
CW, CCW = 0, 1


def ring_kernel(
    chips,
    rows,
    width,
    picks_ref,
    mix_ref,
    tokens_ref,
    gate_ref,
    up_ref,
    down_ref,
    out_ref,
    tok,
    w_gate,
    w_up,
    w_down,
    part,
    sib_part,
    sent,
    got,
    load_sem,
    ag_send,
    ag_recv,
    sib_send,
    sib_recv,
    part_send,
    part_recv,
    rs_send,
    rs_recv,
):
    half_ring = chips // 2
    half = rows // 2
    rep, node, dev = (lax.axis_index(a) for a in ("rep", "node", "dev"))
    odd, along = lax.rem(dev, 2), lax.div(dev, 2)
    here = (1 - odd) * along + odd * (chips - 1 - along)

    def dev_at(position):
        position = lax.rem(position + chips, chips)
        back = lax.div(position, half_ring)
        return (1 - back) * 2 * position + back * (2 * (chips - 1 - position) + 1)

    sibling = (rep, 1 - node, dev)
    onward = ((rep, node, dev_at(here + 1)), (rep, node, dev_at(here - 1)))
    expert = lax.div(node * chips + dev, SHARDS)

    def place(way, distance):
        if distance == 0:
            return 0
        if distance == half_ring:
            return chips - 1
        return 2 * distance - 1 + way

    def gather_copy(step, way, h):
        k = (step * 2 + way) * 2 + h
        return pltpu.make_async_remote_copy(
            src_ref=tok.at[pl.ds(place(way, step) * 2 * rows + h * half, half), :],
            dst_ref=tok.at[pl.ds(place(way, step + 1) * 2 * rows + h * half, half), :],
            send_sem=ag_send.at[k],
            recv_sem=ag_recv.at[k],
            device_id=onward[way],
            device_id_type=MESH,
        )

    def sibling_copy(spot, h):
        k = spot * 2 + h
        return pltpu.make_async_remote_copy(
            src_ref=tok.at[pl.ds(spot * 2 * rows + h * half, half), :],
            dst_ref=tok.at[pl.ds(spot * 2 * rows + rows + h * half, half), :],
            send_sem=sib_send.at[k],
            recv_sem=sib_recv.at[k],
            device_id=sibling,
            device_id_type=MESH,
        )

    def part_copy(spot):
        return pltpu.make_async_remote_copy(
            src_ref=part.at[pl.ds(spot * 2 * rows + rows, rows), :],
            dst_ref=sib_part.at[pl.ds(spot * rows, rows), :],
            send_sem=part_send.at[spot],
            recv_sem=part_recv.at[spot],
            device_id=sibling,
            device_id_type=MESH,
        )

    def scatter_copy(step, way, h):
        k = (step * 2 + way) * 2 + h
        return pltpu.make_async_remote_copy(
            src_ref=sent.at[pl.ds(k * half, half), :],
            dst_ref=got.at[pl.ds(k * half, half), :],
            send_sem=rs_send.at[k],
            recv_sem=rs_recv.at[k],
            device_id=onward[way],
            device_id_type=MESH,
        )

    def crosses(step, way, h):
        return step < half_ring - 1 or way == h

    loads = [
        pltpu.make_async_copy(tokens_ref, tok.at[pl.ds(0, rows), pl.ds(0, width)], load_sem.at[0]),
        pltpu.make_async_copy(gate_ref, w_gate, load_sem.at[1]),
        pltpu.make_async_copy(up_ref, w_up, load_sem.at[2]),
        pltpu.make_async_copy(down_ref, w_down, load_sem.at[3]),
    ]
    for load in loads:
        load.start()

    barrier = pltpu.get_barrier_semaphore()
    for peer in (sibling, onward[CW], onward[CCW]):
        pl.semaphore_signal(barrier, inc=1, device_id=peer, device_id_type=MESH)

    lane = lax.broadcasted_iota(jnp.int32, (rows, LANES), 1)
    lane_expert = lax.rem(lane, LANES // 2)
    dense = jnp.zeros((rows, LANES), jnp.float32)
    for k in range(picks_ref.shape[1]):
        dense += jnp.where(picks_ref[:, k : k + 1] == lane_expert, mix_ref[:, k : k + 1], 0.0)
    high = dense.astype(jnp.bfloat16).astype(jnp.float32)
    low = dense - high
    tok[0:rows, width : width + LANES] = jnp.where(lane < LANES // 2, high, low).astype(
        jnp.bfloat16
    )

    pl.semaphore_wait(barrier, 3)
    loads[0].wait()

    started = []

    def start(copy):
        copy.start()
        started.append(copy)

    def work(spot, count):
        first = spot * 2 * rows
        m = count * 2 * rows
        x = tok[first : first + m, 0:width]
        g = jnp.dot(x, w_gate[...], preferred_element_type=jnp.float32)
        u = jnp.dot(x, w_up[...], preferred_element_type=jnp.float32)
        hidden = (g / (1.0 + jnp.exp(-g)) * u).astype(jnp.bfloat16)
        tail = tok[first : first + m, width : width + LANES].astype(jnp.float32)
        mine = lax.rem(lax.broadcasted_iota(jnp.int32, (m, LANES), 1), LANES // 2) == expert
        weight = jnp.sum(jnp.where(mine, tail, 0.0), axis=1, keepdims=True)
        tile = 512

        @pl.loop(0, width // tile)
        def _(t):
            cols = pl.ds(pl.multiple_of(t * tile, tile), tile)
            o = jnp.dot(hidden, w_down[:, cols], preferred_element_type=jnp.float32)
            part[first : first + m, cols] = (o * weight).astype(jnp.bfloat16)

        for i in range(count):
            start(part_copy(spot + i))

    def add_up(dst, dst_row, spot, h, extra):
        a, b = spot * 2 * rows + h * half, spot * rows + h * half
        tile = 1024

        @pl.loop(0, width // tile)
        def _(t):
            cols = pl.ds(pl.multiple_of(t * tile, tile), tile)
            total = part[a : a + half, cols].astype(jnp.float32)
            total += sib_part[b : b + half, cols].astype(jnp.float32)
            for k in extra:
                total += got[k * half : (k + 1) * half, cols].astype(jnp.float32)
            dst[dst_row : dst_row + half, cols] = total.astype(jnp.bfloat16)

    for h in (0, 1):
        for way in (CW, CCW):
            if crosses(0, way, h):
                start(gather_copy(0, way, h))
    for h in (0, 1):
        start(sibling_copy(0, h))
    for load in loads[1:]:
        load.wait()
    for h in (0, 1):
        sibling_copy(0, h).wait_recv()
    work(0, 1)
    for step in range(1, half_ring):
        for h in (0, 1):
            for way in (CW, CCW):
                gather_copy(step - 1, way, h).wait_recv()
                if crosses(step, way, h):
                    start(gather_copy(step, way, h))
                start(sibling_copy(place(way, step), h))
        for h in (0, 1):
            for way in (CW, CCW):
                sibling_copy(place(way, step), h).wait_recv()
        work(place(CW, step), 2)
    for h in (0, 1):
        gather_copy(half_ring - 1, h, h).wait_recv()
        start(sibling_copy(chips - 1, h))
    for h in (0, 1):
        sibling_copy(chips - 1, h).wait_recv()
    work(chips - 1, 1)

    part_copy(chips - 1).wait_recv()
    for h in (0, 1):
        k = h * 2 + h
        add_up(sent, k * half, chips - 1, h, ())
        start(scatter_copy(0, h, h))
    for step in range(1, half_ring):
        spots = (place(CCW, half_ring - step), place(CW, half_ring - step))
        part_copy(spots[0]).wait_recv()
        part_copy(spots[1]).wait_recv()
        order = [(CW, 0), (CCW, 0), (CW, 1), (CCW, 1)]
        if step == 1:
            order = [(CW, 1), (CCW, 0), (CW, 0), (CCW, 1)]
        for way, h in order:
            extra = ()
            if step > 1 or way == h:
                scatter_copy(step - 1, way, h).wait_recv()
                extra = (((step - 1) * 2 + way) * 2 + h,)
            k = (step * 2 + way) * 2 + h
            add_up(sent, k * half, spots[way], h, extra)
            start(scatter_copy(step, way, h))
    part_copy(0).wait_recv()
    for h in (0, 1):
        extra = []
        for way in (CW, CCW):
            scatter_copy(half_ring - 1, way, h).wait_recv()
            extra.append(((half_ring - 1) * 2 + way) * 2 + h)
        add_up(out_ref, h * half, 0, h, tuple(extra))
    for copy in started:
        copy.wait_send()


def on_ring(tokens, expert_picks, mix_weights, w_gate, w_up, w_down):
    rows, width = tokens.shape
    chips = lax.axis_size("dev")
    ff = w_gate.shape[1]
    wide = width + LANES
    dma = pltpu.SemaphoreType.DMA
    vmem = pl.BlockSpec(memory_space=pltpu.VMEM)
    hbm = pl.BlockSpec(memory_space=pl.ANY)
    bf16 = jnp.bfloat16
    return pl.pallas_call(
        functools.partial(ring_kernel, chips, rows, width),
        out_shape=jax.ShapeDtypeStruct((rows, width), bf16),
        in_specs=[vmem, vmem, hbm, hbm, hbm, hbm],
        out_specs=vmem,
        scratch_shapes=[
            pltpu.VMEM((2 * chips * rows, wide), bf16),
            pltpu.VMEM((width, ff), bf16),
            pltpu.VMEM((width, ff), bf16),
            pltpu.VMEM((ff, width), bf16),
            pltpu.VMEM((2 * chips * rows, width), bf16),
            pltpu.VMEM((chips * rows, width), bf16),
            pltpu.VMEM((chips * rows, width), bf16),
            pltpu.VMEM((chips * rows, width), bf16),
            dma((4,)),
            dma((2 * chips,)),
            dma((2 * chips,)),
            dma((2 * chips,)),
            dma((2 * chips,)),
            dma((chips,)),
            dma((chips,)),
            dma((2 * chips,)),
            dma((2 * chips,)),
        ],
        compiler_params=pltpu.CompilerParams(
            collective_id=0, has_side_effects=True, vmem_limit_bytes=58 * 2**20
        ),
        cost_estimate=pl.CostEstimate(
            flops=2 * 2 * chips * rows * width * ff * 3,
            bytes_accessed=3 * 2 * width * ff,
            transcendentals=2 * chips * rows * ff,
        ),
    )(expert_picks, mix_weights, tokens, w_gate, w_up, w_down)


def on_slots(tokens, expert_picks, mix_weights, w_gate, w_up, w_down):
    rows_here = tokens.shape[0]
    model_width = tokens.shape[1]
    pick_count = expert_picks.shape[1]
    node_count = lax.axis_size("node")
    dev_count = lax.axis_size("dev")
    sources = node_count * dev_count
    experts = sources // SHARDS
    capacity = 2 * rows_here * pick_count // experts
    picks_flat = expert_picks.reshape(-1)
    onehot = (picks_flat[:, None] == jnp.arange(experts, dtype=jnp.int32)[None, :]).astype(
        jnp.int32
    )
    ranking = jnp.cumsum(onehot, axis=0) - onehot
    position = jnp.sum(ranking * onehot, axis=1)
    slot_index = picks_flat * capacity + position
    repeated = jnp.repeat(tokens, pick_count, axis=0)
    outgoing = (
        jnp.zeros((experts * capacity, model_width), jnp.bfloat16).at[slot_index].set(repeated)
    )
    spread = jnp.broadcast_to(
        outgoing.reshape(experts, 1, capacity, model_width),
        (experts, SHARDS, capacity, model_width),
    ).reshape(sources, capacity, model_width)
    incoming = lax.all_to_all(spread, ("node", "dev"), split_axis=0, concat_axis=0, tiled=True)
    leading = incoming.shape[0]
    row_count = incoming.shape[1]
    rows_in = incoming.reshape(leading * row_count, model_width)
    gate_proj = jnp.dot(rows_in, w_gate, preferred_element_type=jnp.float32)
    up_proj = jnp.dot(rows_in, w_up, preferred_element_type=jnp.float32)
    hidden = (jax.nn.silu(gate_proj) * up_proj).astype(jnp.bfloat16)
    shard_out = jnp.dot(hidden, w_down, preferred_element_type=jnp.float32).astype(jnp.bfloat16)
    returned = lax.all_to_all(
        shard_out.reshape(leading, row_count, model_width),
        ("node", "dev"),
        split_axis=0,
        concat_axis=0,
        tiled=True,
    )
    summed = jnp.sum(
        returned.reshape(experts, SHARDS, capacity, model_width).astype(jnp.float32), axis=1
    )
    expert_out = summed.astype(jnp.bfloat16).reshape(experts * capacity, model_width)
    picked = expert_out[slot_index].astype(jnp.float32).reshape(rows_here, pick_count, model_width)
    weighted = picked * mix_weights[:, :, None]
    return jnp.sum(weighted, axis=1).astype(jnp.bfloat16)


def solution(mesh):
    placed = (
        P(("rep", "node", "dev"), None),
        P(("rep", "node", "dev"), None),
        P(("rep", "node", "dev"), None),
        P(None, ("node", "dev")),
        P(None, ("node", "dev")),
        P(("node", "dev"), None),
    )
    sources = mesh.shape["node"] * mesh.shape["dev"]
    few = sources // SHARDS <= 4 and mesh.shape["node"] == 2 and mesh.shape["dev"] % 4 == 0
    return jax.shard_map(
        on_ring if few else on_slots,
        mesh=mesh,
        in_specs=placed,
        out_specs=P(("rep", "node", "dev"), None),
        check_vma=False,
    )
```

```python
import functools

import jax
import jax.numpy as jnp
from jax import lax
from jax.experimental import pallas as pl
from jax.experimental.pallas import tpu as pltpu
from jax.sharding import PartitionSpec as P

SHARDS = 4
LANES = 128
MESH = pl.DeviceIdType.MESH
CW, CCW = 0, 1
LONG = ((CW, 0), (CCW, 1))
SHORT = ((CW, 1), (CCW, 0))


def ring_kernel(
    chips,
    rows,
    width,
    picks_ref,
    mix_ref,
    tokens_ref,
    gate_ref,
    up_ref,
    down_ref,
    out_ref,
    tok,
    w_gate,
    w_up,
    w_down,
    part,
    sib_part,
    sent,
    got,
    load_sem,
    ag_send,
    ag_recv,
    sib_send,
    sib_recv,
    part_send,
    part_recv,
    rs_send,
    rs_recv,
):
    half_ring = chips // 2
    half = rows // 2
    rep, node, dev = (lax.axis_index(a) for a in ("rep", "node", "dev"))
    odd, along = lax.rem(dev, 2), lax.div(dev, 2)
    here = (1 - odd) * along + odd * (chips - 1 - along)

    def dev_at(position):
        position = lax.rem(position + chips, chips)
        back = lax.div(position, half_ring)
        return (1 - back) * 2 * position + back * (2 * (chips - 1 - position) + 1)

    sibling = (rep, 1 - node, dev)
    onward = ((rep, node, dev_at(here + 1)), (rep, node, dev_at(here - 1)))
    expert = lax.div(node * chips + dev, SHARDS)

    def place(way, distance):
        if distance == 0:
            return 0
        if distance == half_ring:
            return chips - 1
        return 2 * distance - 1 + way

    def gather_copy(step, way, h):
        k = (step * 2 + way) * 2 + h
        return pltpu.make_async_remote_copy(
            src_ref=tok.at[pl.ds(place(way, step) * 2 * rows + h * half, half), :],
            dst_ref=tok.at[pl.ds(place(way, step + 1) * 2 * rows + h * half, half), :],
            send_sem=ag_send.at[k],
            recv_sem=ag_recv.at[k],
            device_id=onward[way],
            device_id_type=MESH,
        )

    def sibling_copy(spot, h):
        k = spot * 2 + h
        return pltpu.make_async_remote_copy(
            src_ref=tok.at[pl.ds(spot * 2 * rows + h * half, half), :],
            dst_ref=tok.at[pl.ds(spot * 2 * rows + rows + h * half, half), :],
            send_sem=sib_send.at[k],
            recv_sem=sib_recv.at[k],
            device_id=sibling,
            device_id_type=MESH,
        )

    def part_copy(spot):
        return pltpu.make_async_remote_copy(
            src_ref=part.at[pl.ds(spot * 2 * rows + rows, rows), :],
            dst_ref=sib_part.at[pl.ds(spot * rows, rows), :],
            send_sem=part_send.at[spot],
            recv_sem=part_recv.at[spot],
            device_id=sibling,
            device_id_type=MESH,
        )

    def scatter_copy(step, way, h):
        k = (step * 2 + way) * 2 + h
        return pltpu.make_async_remote_copy(
            src_ref=sent.at[pl.ds(k * half, half), :],
            dst_ref=got.at[pl.ds(k * half, half), :],
            send_sem=rs_send.at[k],
            recv_sem=rs_recv.at[k],
            device_id=onward[way],
            device_id_type=MESH,
        )

    def crosses(step, way, h):
        return step < half_ring - 1 or way == h

    loads = [
        pltpu.make_async_copy(tokens_ref, tok.at[pl.ds(0, rows), pl.ds(0, width)], load_sem.at[0]),
        pltpu.make_async_copy(gate_ref, w_gate, load_sem.at[1]),
        pltpu.make_async_copy(up_ref, w_up, load_sem.at[2]),
        pltpu.make_async_copy(down_ref, w_down, load_sem.at[3]),
    ]
    for load in loads:
        load.start()

    barrier = pltpu.get_barrier_semaphore()
    for peer in (sibling, onward[CW], onward[CCW]):
        pl.semaphore_signal(barrier, inc=1, device_id=peer, device_id_type=MESH)

    line = lax.broadcasted_iota(jnp.int32, (LANES, rows), 0)
    line_expert = lax.rem(line, LANES // 2)
    dense = jnp.zeros((LANES, rows), jnp.float32)
    for k in range(picks_ref.shape[0]):
        dense += jnp.where(picks_ref[k : k + 1, :] == line_expert, mix_ref[k : k + 1, :], 0.0)
    high = dense.astype(jnp.bfloat16).astype(jnp.float32)
    low = dense - high
    both = jnp.where(line < LANES // 2, high, low)
    tok[0:rows, width : width + LANES] = both.T.astype(jnp.bfloat16)

    pl.semaphore_wait(barrier, 3)
    loads[0].wait()

    started = []

    def start(copy):
        copy.start()
        started.append(copy)

    def work(spot, count):
        first = spot * 2 * rows
        m = count * 2 * rows
        x = tok[first : first + m, 0:width]
        g = jnp.dot(x, w_gate[...], preferred_element_type=jnp.float32)
        u = jnp.dot(x, w_up[...], preferred_element_type=jnp.float32)
        hidden = (g / (1.0 + jnp.exp(-g)) * u).astype(jnp.bfloat16)
        tail = tok[first : first + m, width : width + LANES].astype(jnp.float32)
        mine = lax.rem(lax.broadcasted_iota(jnp.int32, (m, LANES), 1), LANES // 2) == expert
        weight = jnp.sum(jnp.where(mine, tail, 0.0), axis=1, keepdims=True)
        tile = 512

        @pl.loop(0, width // tile)
        def _(t):
            cols = pl.ds(pl.multiple_of(t * tile, tile), tile)
            o = jnp.dot(hidden, w_down[:, cols], preferred_element_type=jnp.float32)
            part[first : first + m, cols] = (o * weight).astype(jnp.bfloat16)

        for i in range(count):
            start(part_copy(spot + i))

    def add_up(dst, dst_row, spot, h, extra):
        a, b = spot * 2 * rows + h * half, spot * rows + h * half
        tile = 1024

        @pl.loop(0, width // tile)
        def _(t):
            cols = pl.ds(pl.multiple_of(t * tile, tile), tile)
            total = part[a : a + half, cols].astype(jnp.float32)
            total += sib_part[b : b + half, cols].astype(jnp.float32)
            for k in extra:
                total += got[k * half : (k + 1) * half, cols].astype(jnp.float32)
            dst[dst_row : dst_row + half, cols] = total.astype(jnp.bfloat16)

    def pass_on(step, chain):
        for way, h in chain:
            spot = place(1 - way, half_ring - step)
            if chain is SHORT:
                part_copy(spot).wait_recv()
            extra = ()
            if step > 1 or way == h:
                scatter_copy(step - 1, way, h).wait_recv()
                extra = (((step - 1) * 2 + way) * 2 + h,)
            k = (step * 2 + way) * 2 + h
            add_up(sent, k * half, spot, h, extra)
            start(scatter_copy(step, way, h))

    for way, h in LONG + SHORT:
        if crosses(0, way, h):
            start(gather_copy(0, way, h))
    for h in (0, 1):
        start(sibling_copy(0, h))
    for load in loads[1:]:
        load.wait()
    for h in (0, 1):
        sibling_copy(0, h).wait_recv()
    work(0, 1)
    for step in range(1, half_ring):
        for way, h in LONG + SHORT:
            gather_copy(step - 1, way, h).wait_recv()
            if crosses(step, way, h):
                start(gather_copy(step, way, h))
            start(sibling_copy(place(way, step), h))
        for h in (0, 1):
            for way in (CW, CCW):
                sibling_copy(place(way, step), h).wait_recv()
        work(place(CW, step), 2)
    for way, h in LONG:
        gather_copy(half_ring - 1, way, h).wait_recv()
        start(sibling_copy(chips - 1, h))
    pass_on(1, SHORT)
    for h in (0, 1):
        sibling_copy(chips - 1, h).wait_recv()
    work(chips - 1, 1)

    if half_ring > 2:
        pass_on(2, SHORT)
    part_copy(chips - 1).wait_recv()
    for h in (0, 1):
        add_up(sent, (h * 2 + h) * half, chips - 1, h, ())
        start(scatter_copy(0, h, h))
    for step in range(1, half_ring):
        pass_on(step, LONG)
        if step + 2 < half_ring:
            pass_on(step + 2, SHORT)
    part_copy(0).wait_recv()
    for h in (0, 1):
        extra = []
        for way in (CW, CCW):
            scatter_copy(half_ring - 1, way, h).wait_recv()
            extra.append(((half_ring - 1) * 2 + way) * 2 + h)
        add_up(out_ref, h * half, 0, h, tuple(extra))
    for copy in started:
        copy.wait_send()


def on_ring(tokens, expert_picks, mix_weights, w_gate, w_up, w_down):
    rows, width = tokens.shape
    chips = lax.axis_size("dev")
    ff = w_gate.shape[1]
    wide = width + LANES
    dma = pltpu.SemaphoreType.DMA
    vmem = pl.BlockSpec(memory_space=pltpu.VMEM)
    hbm = pl.BlockSpec(memory_space=pl.ANY)
    bf16 = jnp.bfloat16
    return pl.pallas_call(
        functools.partial(ring_kernel, chips, rows, width),
        out_shape=jax.ShapeDtypeStruct((rows, width), bf16),
        in_specs=[vmem, vmem, hbm, hbm, hbm, hbm],
        out_specs=vmem,
        scratch_shapes=[
            pltpu.VMEM((2 * chips * rows, wide), bf16),
            pltpu.VMEM((width, ff), bf16),
            pltpu.VMEM((width, ff), bf16),
            pltpu.VMEM((ff, width), bf16),
            pltpu.VMEM((2 * chips * rows, width), bf16),
            pltpu.VMEM((chips * rows, width), bf16),
            pltpu.VMEM((chips * rows, width), bf16),
            pltpu.VMEM((chips * rows, width), bf16),
            dma((4,)),
            dma((2 * chips,)),
            dma((2 * chips,)),
            dma((2 * chips,)),
            dma((2 * chips,)),
            dma((chips,)),
            dma((chips,)),
            dma((2 * chips,)),
            dma((2 * chips,)),
        ],
        compiler_params=pltpu.CompilerParams(
            collective_id=0, has_side_effects=True, vmem_limit_bytes=58 * 2**20
        ),
        cost_estimate=pl.CostEstimate(
            flops=2 * 2 * chips * rows * width * ff * 3,
            bytes_accessed=3 * 2 * width * ff,
            transcendentals=2 * chips * rows * ff,
        ),
    )(expert_picks.T, mix_weights.T, tokens, w_gate, w_up, w_down)


def on_slots(tokens, expert_picks, mix_weights, w_gate, w_up, w_down):
    rows_here = tokens.shape[0]
    model_width = tokens.shape[1]
    pick_count = expert_picks.shape[1]
    node_count = lax.axis_size("node")
    dev_count = lax.axis_size("dev")
    sources = node_count * dev_count
    experts = sources // SHARDS
    capacity = 2 * rows_here * pick_count // experts
    picks_flat = expert_picks.reshape(-1)
    onehot = (picks_flat[:, None] == jnp.arange(experts, dtype=jnp.int32)[None, :]).astype(
        jnp.int32
    )
    ranking = jnp.cumsum(onehot, axis=0) - onehot
    position = jnp.sum(ranking * onehot, axis=1)
    slot_index = picks_flat * capacity + position
    repeated = jnp.repeat(tokens, pick_count, axis=0)
    outgoing = (
        jnp.zeros((experts * capacity, model_width), jnp.bfloat16).at[slot_index].set(repeated)
    )
    spread = jnp.broadcast_to(
        outgoing.reshape(experts, 1, capacity, model_width),
        (experts, SHARDS, capacity, model_width),
    ).reshape(sources, capacity, model_width)
    incoming = lax.all_to_all(spread, ("node", "dev"), split_axis=0, concat_axis=0, tiled=True)
    leading = incoming.shape[0]
    row_count = incoming.shape[1]
    rows_in = incoming.reshape(leading * row_count, model_width)
    gate_proj = jnp.dot(rows_in, w_gate, preferred_element_type=jnp.float32)
    up_proj = jnp.dot(rows_in, w_up, preferred_element_type=jnp.float32)
    hidden = (jax.nn.silu(gate_proj) * up_proj).astype(jnp.bfloat16)
    shard_out = jnp.dot(hidden, w_down, preferred_element_type=jnp.float32).astype(jnp.bfloat16)
    returned = lax.all_to_all(
        shard_out.reshape(leading, row_count, model_width),
        ("node", "dev"),
        split_axis=0,
        concat_axis=0,
        tiled=True,
    )
    summed = jnp.sum(
        returned.reshape(experts, SHARDS, capacity, model_width).astype(jnp.float32), axis=1
    )
    expert_out = summed.astype(jnp.bfloat16).reshape(experts * capacity, model_width)
    picked = expert_out[slot_index].astype(jnp.float32).reshape(rows_here, pick_count, model_width)
    weighted = picked * mix_weights[:, :, None]
    return jnp.sum(weighted, axis=1).astype(jnp.bfloat16)


def solution(mesh):
    placed = (
        P(("rep", "node", "dev"), None),
        P(("rep", "node", "dev"), None),
        P(("rep", "node", "dev"), None),
        P(None, ("node", "dev")),
        P(None, ("node", "dev")),
        P(("node", "dev"), None),
    )
    sources = mesh.shape["node"] * mesh.shape["dev"]
    few = sources // SHARDS <= 4 and mesh.shape["node"] == 2 and mesh.shape["dev"] % 4 == 0
    return jax.shard_map(
        on_ring if few else on_slots,
        mesh=mesh,
        in_specs=placed,
        out_specs=P(("rep", "node", "dev"), None),
        check_vma=False,
    )
```
